32 devices in a mesh: freq: 2 (over y), src: 8 (over z, x), rcv: 2 (over core).
Axes of the slice: x: 2, y: 2, z: 4, core: 2. Of those that a mesh axis runs over, the one named last changes fastest.
Arguments:
- panel: float32 [4, 1024, 5632], P('freq', 'src', 'rcv'), parts along dimension 0, may hold values from -6 to 6
- obliquity: float32 [4, 131072], P('freq'), parts along dimension 0, may hold values from -0.125 to 0.125
- panel_stations: int32 [1024], replicated, may hold values from 0 to 131071
- tile_map: int32 [512, 2], P('freq'), parts along dimension 0, may hold values from -1 to 21, as said below
- recorded: float32 [256, 4, 256, 256], P(('src', 'rcv'), 'freq'), parts along dimension 1, may hold values from -6 to 6
Outputs:
- demultiple: float32 [256, 4, 256, 256], P(('src', 'rcv'), 'freq'), parts along dimension 1
The draws below stay inside these ranges and needn't reach their ends.
There are 2 independent parts, one for each index of `freq`. The reference program is written for one: setup_inputs(seed, part) draws one part's arguments, and reference() takes and returns one part's arrays. A program takes and returns all parts, laid end to end along the dimension named above; an argument that names none is the same for every part. Nothing has to cross between parts.
Inputs may be any that keep to these rules, and one draw needn't show every extreme that they name: `tile_map`: each slot holds a row tile i and a column tile j with j <= i; each of the 253 such tiles stands in exactly one slot; remaining slots hold -1 in both entries.
All inputs are finite; a program needn't handle non-finite values.
Results may differ from the reference program's by a relative error of at most 0.0044.
Values may be sent and summed in bfloat16 or wider, within the bound.
No kernel may reach another device: no remote copies, remote signals or barrier semaphores. Data moves between devices by JAX's collectives and lax.ppermute only.
A program may use at most 192 MiB of HBM per device.

```python
import jax
import jax.numpy as jnp
import numpy as np
from jax import lax

TB = 256
G = 22
NSTAT = 131072
K = 1024
NW = 5632
DEVS_PART = 16
TILE_DEV = 16
SLOTS = 256


def draw_tile_map(key, part):
    rows_np, cols_np = np.tril_indices(G)
    nlow = G * (G + 1) // 2
    order = jax.random.permutation(key, nlow)
    rank = jnp.arange(nlow, dtype=jnp.int32)
    slot = rank % DEVS_PART * TILE_DEV + rank // DEVS_PART
    pairs = jnp.stack([jnp.asarray(rows_np, dtype=jnp.int32)[order], jnp.asarray(cols_np, dtype=jnp.int32)[order]], axis=1)
    filled = jnp.full((SLOTS, 2), -1, dtype=jnp.int32)
    return filled.at[slot].set(pairs)


def with_ends(result, rng, low, top_value):
    index_at = [jax.random.randint(jax.random.fold_in(rng, axis), (), 0, length) for axis, length in enumerate(result.shape)]
    main_axis = result.shape.index(max(result.shape))
    neighbour = index_at[:main_axis] + [(index_at[main_axis] + 1) % result.shape[main_axis]] + index_at[main_axis + 1:]
    return result.at[tuple(index_at)].set(low).at[tuple(neighbour)].set(top_value)


def level_of(stream_key, dims, pieces, smallest, largest):
    gain = 1.0
    for position, blocks in pieces:
        steps = jax.random.uniform(jax.random.fold_in(jax.random.fold_in(stream_key, 6), position), (blocks,), jnp.float32, smallest / len(pieces), largest / len(pieces))
        gain = gain * jnp.repeat(jnp.exp(steps), dims[position] // blocks).reshape((-1,) + (1,) * (len(dims) - 1 - position))
    return gain


def noise(stream_key, extent, width, limit, cuts=(), held_as=jnp.bfloat16):
    drawn = jax.random.normal(stream_key, extent, jnp.float32) * width
    if len(cuts) > 0:
        drawn = level_of(stream_key, extent, cuts, -0.22, 0.18) * drawn
    return jnp.clip(drawn, min=-limit, max=limit).astype(held_as)


def setup_inputs(seed: int = 0, part: int = 0) -> dict:
    streams_of = jax.random.split(jax.random.key(seed), 6)
    part_splits = jax.random.split(jax.random.fold_in(streams_of[5], part), 6)
    panel = noise(part_splits[0], (2, K, NW), 1.0, 6.0, ((1, 8), (2, 2)), jnp.float32)
    obliquity = noise(part_splits[1], (2, NSTAT), (2 * K) ** -0.5, 0.125, (), jnp.float32)
    panel_stations = with_ends(jax.random.randint(streams_of[2], (K,), 0, NSTAT), jax.random.fold_in(streams_of[2], 1), 0, NSTAT - 1).astype(jnp.int32)
    tile_map = draw_tile_map(jax.random.fold_in(jax.random.fold_in(streams_of[5], part), 71), part)
    recorded = noise(part_splits[4], (SLOTS, 2, TB, TB), 1.0, 6.0, ((0, 16),), jnp.float32)
    return dict(panel=panel, obliquity=obliquity, panel_stations=panel_stations, tile_map=tile_map, recorded=recorded)


def reference(panel, obliquity, panel_stations, tile_map, recorded):
    weight_k = jnp.take(obliquity, panel_stations, axis=1)
    panel_b = panel.astype(jnp.bfloat16).astype(jnp.float32)
    w_real = weight_k[0][:, None]
    w_imag = weight_k[1][:, None]
    weighted = jnp.stack([w_real * panel_b[0] - w_imag * panel_b[1], w_real * panel_b[1] + w_imag * panel_b[0]])
    weighted = weighted.astype(jnp.bfloat16).astype(jnp.float32)
    hp = lax.Precision.HIGHEST

    def one_slot(slot):
        row_tile = tile_map[slot, 0]
        col_tile = tile_map[slot, 1]
        valid = (row_tile >= 0).astype(jnp.float32)
        row_start = (jnp.maximum(row_tile, 0) * TB).astype(jnp.int32)
        col_start = (jnp.maximum(col_tile, 0) * TB).astype(jnp.int32)
        left = lax.dynamic_slice_in_dim(weighted, row_start, TB, 2)
        right = lax.dynamic_slice_in_dim(panel_b, col_start, TB, 2)
        real_part = jnp.dot(left[0].T, right[0], precision=hp) - jnp.dot(left[1].T, right[1], precision=hp)
        imag_part = jnp.dot(left[0].T, right[1], precision=hp) + jnp.dot(left[1].T, right[0], precision=hp)
        return recorded[slot] - valid * jnp.stack([real_part, imag_part])

    return lax.map(one_slot, jnp.arange(SLOTS, dtype=jnp.int32))
```

```python
import functools

import jax
import jax.numpy as jnp
from jax import lax
from jax.experimental import pallas as pl
from jax.experimental.pallas import tpu as pltpu
from jax.sharding import PartitionSpec as P

TN = (((0,), (0,)), ((), ()))


def tile_kernel(rows_ref, cols_ref, valid_ref, weight_ref, left_ref, right_ref, recorded_ref, out_ref):
    slot = pl.program_id(0)
    depth = left_ref.shape[0] * left_ref.shape[3]
    side = left_ref.shape[4]
    left_real = left_ref[:, 0, 0].reshape(depth, side).astype(jnp.float32)
    left_imag = left_ref[:, 0, 1].reshape(depth, side).astype(jnp.float32)
    w_real = weight_ref[0]
    w_imag = weight_ref[1]
    real_w = (w_real * left_real - w_imag * left_imag).astype(jnp.bfloat16)
    imag_w = (w_real * left_imag + w_imag * left_real).astype(jnp.bfloat16)
    right_real = right_ref[:, 0, 0].reshape(depth, side)
    right_imag = right_ref[:, 0, 1].reshape(depth, side)
    dot = functools.partial(lax.dot_general, dimension_numbers=TN, preferred_element_type=jnp.float32)
    real = dot(real_w, right_real) - dot(imag_w, right_imag)
    imag = dot(real_w, right_imag) + dot(imag_w, right_real)
    scale = valid_ref[slot].astype(jnp.float32)
    out_ref[0, 0] = recorded_ref[0, 0] - scale * real
    out_ref[0, 1] = recorded_ref[0, 1] - scale * imag


def tile_products(gathered, weight, rows, cols, valid, recorded):
    n_src, n_rcv, parts, depth, width = gathered.shape
    slots, _, side, _ = recorded.shape
    per_half = width // side
    half = (n_src, 1, parts, depth, side)
    flops = 8 * slots * side * side * n_src * depth
    return pl.pallas_call(
        tile_kernel,
        grid_spec=pltpu.PrefetchScalarGridSpec(
            num_scalar_prefetch=3,
            grid=(slots,),
            in_specs=[
                pl.BlockSpec((2, n_src * depth, side), lambda s, r, c, v: (0, 0, 0)),
                pl.BlockSpec(half, lambda s, r, c, v: (0, r[s] // per_half, 0, 0, r[s] % per_half)),
                pl.BlockSpec(half, lambda s, r, c, v: (0, c[s] // per_half, 0, 0, c[s] % per_half)),
                pl.BlockSpec((1, 2, side, side), lambda s, r, c, v: (s, 0, 0, 0)),
            ],
            out_specs=pl.BlockSpec((1, 2, side, side), lambda s, r, c, v: (s, 0, 0, 0)),
        ),
        out_shape=jax.ShapeDtypeStruct(recorded.shape, jnp.float32),
        compiler_params=pltpu.CompilerParams(vmem_limit_bytes=48 * 2**20),
        cost_estimate=pl.CostEstimate(flops=flops, bytes_accessed=50 * 2**20, transcendentals=0),
    )(rows, cols, valid, weight, gathered, gathered, recorded)


def body(panel, obliquity, panel_stations, tile_map, recorded):
    n_src = lax.axis_size("src")
    n_rcv = lax.axis_size("rcv")
    slots = recorded.shape[0]
    side = recorded.shape[2]
    gathered = lax.all_gather(panel.astype(jnp.bfloat16), ("src", "rcv"))
    gathered = gathered.reshape((n_src, n_rcv) + panel.shape)
    weight = jnp.take(obliquity, panel_stations, axis=1)
    weight = jnp.broadcast_to(weight[:, :, None], weight.shape + (side,))
    own = lax.axis_index("src") * n_rcv + lax.axis_index("rcv")
    mine = lax.dynamic_slice_in_dim(tile_map, own * slots, slots, 0)
    valid = (mine[:, 0] >= 0).astype(jnp.int32)
    rows = jnp.maximum(mine[:, 0], 0)
    cols = jnp.maximum(mine[:, 1], 0)
    return tile_products(gathered, weight, rows, cols, valid, recorded)


def solution(mesh):
    return jax.shard_map(
        body,
        mesh=mesh,
        in_specs=(
            P("freq", "src", "rcv"),
            P("freq", None),
            P(),
            P("freq", None),
            P(("src", "rcv"), "freq", None, None),
        ),
        out_specs=P(("src", "rcv"), "freq", None, None),
        check_vma=False,
    )
```

```python
import functools

import jax
import jax.numpy as jnp
from jax import lax
from jax.experimental import pallas as pl
from jax.experimental.pallas import tpu as pltpu
from jax.sharding import PartitionSpec as P

LANES = 128
COST = 1000
LIMIT = 16
GROUP = 2
ANY = pl.BlockSpec(memory_space=pl.ANY)
together = lax.optimization_barrier


def turn_kernel(_, kept_in, given_in, kept_out, given_out):
    for in_ref, out_ref in ((kept_in, kept_out), (given_in, given_out)):
        block = in_ref[...]
        out_ref[...] = block.reshape(block.shape[0] * block.shape[1], block.shape[2]).T.astype(jnp.bfloat16)


def turn(panel, rcv):
    parts, depth, width = panel.shape
    depth = depth // 2
    cols = width // 2
    out = jax.ShapeDtypeStruct((width, parts * depth), jnp.bfloat16)
    return pl.pallas_call(
        turn_kernel,
        grid_spec=pltpu.PrefetchScalarGridSpec(
            num_scalar_prefetch=1,
            grid=(width // cols,),
            in_specs=[
                pl.BlockSpec((parts, depth, cols), lambda c, r: (0, r[0], c)),
                pl.BlockSpec((parts, depth, cols), lambda c, r: (0, 1 - r[0], c)),
            ],
            out_specs=[pl.BlockSpec((cols, parts * depth), lambda c, r: (c, 0))] * 2,
        ),
        out_shape=[out, out],
        cost_estimate=pl.CostEstimate(flops=0, bytes_accessed=6 * panel.size, transcendentals=0),
    )(rcv[None], panel, panel)


def weights_kernel(stations_ref, line_ref, out_ref, table, sem):
    copies = [pltpu.make_async_copy(line_ref.at[:, part], table.at[part], sem.at[part]) for part in range(2)]
    for copy in copies:
        copy.start()
    stations = stations_ref[...]
    n_blocks = table.shape[1]
    block = lax.broadcasted_iota(jnp.int32, (n_blocks, stations.shape[1]), 0)
    pick = (block == stations // LANES).astype(jnp.float32).astype(jnp.bfloat16)
    lane = lax.broadcasted_iota(jnp.int32, (LANES, stations.shape[1]), 0)
    here = lane == stations % LANES
    for part in range(2):
        copies[part].wait()
        rest = table[part]
        total = None
        for _ in range(3):
            piece = rest.astype(jnp.bfloat16)
            rest = rest - piece.astype(jnp.float32)
            got = lax.dot_general(piece, pick, (((0,), (0,)), ((), ())), preferred_element_type=jnp.float32)
            total = got if total is None else total + got
        out_ref[pl.ds(part, 1), :] = jnp.sum(jnp.where(here, total, 0.0), axis=0, keepdims=True)


def station_weights(obliquity, stations):
    parts, line = obliquity.shape
    table = obliquity.reshape(parts, line // LANES, LANES).transpose(1, 0, 2)
    count = stations.shape[0]
    return pl.pallas_call(
        weights_kernel,
        in_specs=[pl.BlockSpec(memory_space=pltpu.VMEM), ANY],
        out_specs=pl.BlockSpec(memory_space=pltpu.VMEM),
        out_shape=jax.ShapeDtypeStruct((parts, count), jnp.float32),
        scratch_shapes=[pltpu.VMEM((parts, line // LANES, LANES), jnp.float32), pltpu.SemaphoreType.DMA((parts,))],
        compiler_params=pltpu.CompilerParams(vmem_limit_bytes=32 * 2**20),
        cost_estimate=pl.CostEstimate(flops=12 * line * count, bytes_accessed=4 * parts * line, transcendentals=0),
    )(stations[None, :], table)


def tiles_kernel(places, form, rows_ref, cols_ref, valid_ref, at_ref, *refs):
    n = len(places)
    pieces = refs[: 2 * n]
    weight_ref = refs[2 * n]
    refs = refs[2 * n + 1 :]
    acc_ref = got_ref = sem = None
    if form == "start":
        _, out_ref, token_ref = refs
    elif form == "last":
        acc_ref, got_ref, _, result_ref, out_ref, sem = refs
    else:
        acc_ref, _, out_ref, token_ref = refs
    if form != "last":
        token_ref[...] = jnp.zeros_like(token_ref)
    slots, _, side, _ = out_ref.shape
    per_half = pieces[0].shape[0] // side
    rcv = at_ref[0]
    shard = at_ref[1]
    half_lane = lax.broadcasted_iota(jnp.int32, (1, LANES), 1) < LANES // 2
    sign = jnp.where(half_lane, 1.0, -1.0)
    w_at = [lax.bitwise_xor(shard, relative) * 2 + lax.bitwise_xor(rcv, other) for relative, other in places]
    w_real = [weight_ref[0, pl.ds(index, 1), :] for index in w_at]
    w_imag = [weight_ref[1, pl.ds(index, 1), :] for index in w_at]

    def panel(piece, tile):
        place = pl.ds(pl.multiple_of(lax.rem(tile, per_half) * side, side), side)
        return jnp.where(tile // per_half == rcv, pieces[2 * piece][place, :], pieces[2 * piece + 1][place, :])

    def one_slot(slot):
        row = rows_ref[slot]
        col = cols_ref[slot]
        scale = valid_ref[slot].astype(jnp.float32)
        both = None
        for first in range(0, n, GROUP):
            upper, lower, right = [], [], []
            for p in range(first, min(first + GROUP, n)):
                value = panel(p, row).astype(jnp.float32)
                weighted = value * w_real[p] + pltpu.roll(value, LANES // 2, 1) * w_imag[p]
                upper.append((weighted * sign).astype(jnp.bfloat16))
                lower.append(pltpu.roll(weighted, LANES // 2, 1).astype(jnp.bfloat16))
                right.append(panel(p, col))
            left = jnp.concatenate([jnp.concatenate(upper, 1), jnp.concatenate(lower, 1)], 0)
            part = lax.dot_general(
                left, jnp.concatenate(right, 1), (((1,), (1,)), ((), ())), preferred_element_type=jnp.float32
            )
            both = part if both is None else both + part
        for part in range(2):
            value = -scale * both[part * side : (part + 1) * side]
            if acc_ref is not None:
                value = acc_ref[slot, part] + value
            if got_ref is not None:
                value = value + got_ref[slot, part].astype(jnp.float32)
            out_ref[slot, part] = value.astype(out_ref.dtype)
        if form == "last":
            pltpu.make_async_copy(out_ref.at[slot], result_ref.at[slot], sem.at[slot]).start()

    unroll = 4 if slots % 4 == 0 else 1

    @pl.loop(0, slots // unroll)
    def _(step):
        for i in range(unroll):
            one_slot(step * unroll + i)

    if form == "last":

        @pl.loop(0, slots)
        def _(slot):
            pltpu.make_async_copy(out_ref.at[slot], result_ref.at[slot], sem.at[slot]).wait()


def subtract(form, pieces, scalars, weights, shape, token, acc=None, got=None):
    n = len(pieces)
    places = [piece[:2] for piece in pieces]
    operands = [array for piece in pieces for array in piece[2:]] + [weights]
    operands += [array for array in (acc, got) if array is not None] + [token]
    vmem = pl.BlockSpec(memory_space=pltpu.VMEM)
    last = form == "last"
    result = jax.ShapeDtypeStruct(shape, jnp.float32)
    if form == "give":
        result = jax.ShapeDtypeStruct(shape, jnp.bfloat16)
    elif not last:
        result = pltpu.VMEM(shape, jnp.float32)
    return pl.pallas_call(
        functools.partial(tiles_kernel, places, form),
        in_specs=[pl.BlockSpec(memory_space=pltpu.SMEM)] * 4 + [vmem] * len(operands),
        out_specs=ANY if last else [vmem, vmem],
        scratch_shapes=[pltpu.VMEM(shape, jnp.float32), pltpu.SemaphoreType.DMA((shape[0],))] if last else [],
        out_shape=result if last else [result, jax.ShapeDtypeStruct((8, LANES), jnp.float32)],
        input_output_aliases={4 + 2 * n + 1: 0} if form == "add" else {},
        compiler_params=pltpu.CompilerParams(vmem_limit_bytes=LIMIT * 2**20),
        cost_estimate=pl.CostEstimate(flops=COST, bytes_accessed=COST, transcendentals=0),
    )(*scalars, *operands)


def body(panel, obliquity, panel_stations, tile_map, recorded):
    n_src = lax.axis_size("src")
    n_rcv = lax.axis_size("rcv")
    rcv = lax.axis_index("rcv")
    src = lax.axis_index("src")
    slots = recorded.shape[0]
    shards = 8
    span = n_src // shards
    if span > 1:
        groups = [[g * span + i for i in range(span)] for g in range(shards)]
        near = lax.all_gather(panel.astype(jnp.bfloat16), "src", axis=1, tiled=True, axis_index_groups=groups)
        panel = near.astype(jnp.float32)

    def send(a, distance):
        return lax.ppermute(a, "src", [(i, i ^ (distance * span)) for i in range(n_src)])

    def swap(a):
        return lax.ppermute(a, "rcv", [(0, 1), (1, 0)])

    def slots_of(device):
        mine = lax.dynamic_slice_in_dim(tile_map, device * slots, slots, 0)
        valid = (mine[:, 0] >= 0).astype(jnp.int32)
        place = jnp.stack([rcv, src // span]).astype(jnp.int32)
        return jnp.maximum(mine[:, 0], 0), jnp.maximum(mine[:, 1], 0), valid, place

    mine = slots_of(src * n_rcv + rcv)
    theirs = slots_of(src * n_rcv + 1 - rcv)
    w = station_weights(obliquity, panel_stations).reshape(2, shards * 2, -1)
    weights = jnp.stack([jnp.concatenate([w[0], w[0]], -1), jnp.concatenate([-w[1], w[1]], -1)])
    shape = recorded.shape
    token = jnp.zeros((8, LANES), jnp.float32)

    X, Z1, Z2 = 1, 2, 4
    h0, give = turn(panel, rcv)
    h1 = swap(give)
    A0 = send(h0, Z1)
    B0 = send(h0, Z2)
    X0 = send(h0, X)
    X1 = send(h1, X)
    A0, B0, X0, X1, h1, weights = together((A0, B0, X0, X1, h1, weights))

    A1 = send(h1, Z1)
    B1 = send(h1, Z2)
    XA0 = send(A0, X)
    XB0 = send(B0, X)
    pieces = [(0, 0, h0, h1), (X, 0, X0, X1)]
    away, token = subtract("start", pieces, theirs, weights, shape, token)
    home, token = subtract("first", pieces, mine, weights, shape, token, recorded)
    A1, B1, XA0, XB0, token = together((A1, B1, XA0, XB0, token))

    ZZ0 = send(B0, Z1)
    ZZ1 = send(B1, Z1)
    XB1 = send(B1, X)
    XA1 = send(A1, X)
    pieces = [(Z1, 0, A0, A1), (Z2, 0, B0, B1)]
    away, token = subtract("add", pieces, theirs, weights, shape, token, away)
    home, token = subtract("add", pieces, mine, weights, shape, token, home)
    ZZ0, ZZ1, XB1, XA1, token = together((ZZ0, ZZ1, XB1, XA1, token))

    XZZ0 = send(ZZ0, X)
    ZXB1 = send(XB1, Z1)
    pieces = [(Z1 + Z2, 0, ZZ0, ZZ1), (X + Z1, 0, XA0, XA1), (X + Z2, 0, XB0, XB1)]
    away, token = subtract("give", pieces, theirs, weights, shape, token, away)
    got = swap(away)
    home, token = subtract("add", pieces, mine, weights, shape, token, home)
    XZZ0, ZXB1, token = together((XZZ0, ZXB1, token))

    far = X + Z1 + Z2
    pieces = [(far, 0, XZZ0, ZXB1), (far, 1, swap(ZXB1), swap(XZZ0))]
    return subtract("last", pieces, mine, weights, shape, token, home, got)


def solution(mesh):
    return jax.shard_map(
        body,
        mesh=mesh,
        in_specs=(
            P("freq", "src", "rcv"),
            P("freq", None),
            P(),
            P("freq", None),
            P(("src", "rcv"), "freq", None, None),
        ),
        out_specs=P(("src", "rcv"), "freq", None, None),
        check_vma=False,
    )
```

```python
import functools

import jax
import jax.numpy as jnp
from jax import lax
from jax.experimental import pallas as pl
from jax.experimental.pallas import tpu as pltpu
from jax.sharding import PartitionSpec as P

LANES = 128
COST = 1000
LIMIT = 16
GROUP = 2
ANY = pl.BlockSpec(memory_space=pl.ANY)
together = lax.optimization_barrier


def turn_kernel(_, kept_in, given_in, kept_out, given_out):
    for in_ref, out_ref in ((kept_in, kept_out), (given_in, given_out)):
        block = in_ref[...]
        out_ref[...] = block.reshape(block.shape[0] * block.shape[1], block.shape[2]).T.astype(jnp.bfloat16)


def turn(panel, rcv):
    parts, depth, width = panel.shape
    depth = depth // 2
    cols = width // 2
    out = jax.ShapeDtypeStruct((width, parts * depth), jnp.bfloat16)
    return pl.pallas_call(
        turn_kernel,
        grid_spec=pltpu.PrefetchScalarGridSpec(
            num_scalar_prefetch=1,
            grid=(width // cols,),
            in_specs=[
                pl.BlockSpec((parts, depth, cols), lambda c, r: (0, r[0], c)),
                pl.BlockSpec((parts, depth, cols), lambda c, r: (0, 1 - r[0], c)),
            ],
            out_specs=[pl.BlockSpec((cols, parts * depth), lambda c, r: (c, 0))] * 2,
        ),
        out_shape=[out, out],
        cost_estimate=pl.CostEstimate(flops=0, bytes_accessed=6 * panel.size, transcendentals=0),
    )(rcv[None], panel, panel)


def weights_kernel(stations_ref, line_ref, out_ref, table, sem):
    copies = [pltpu.make_async_copy(line_ref.at[:, part], table.at[part], sem.at[part]) for part in range(2)]
    for copy in copies:
        copy.start()
    stations = stations_ref[...]
    n_blocks = table.shape[1]
    block = lax.broadcasted_iota(jnp.int32, (n_blocks, stations.shape[1]), 0)
    pick = (block == stations // LANES).astype(jnp.float32).astype(jnp.bfloat16)
    lane = lax.broadcasted_iota(jnp.int32, (LANES, stations.shape[1]), 0)
    here = lane == stations % LANES
    for part in range(2):
        copies[part].wait()
        rest = table[part]
        total = None
        for _ in range(3):
            piece = rest.astype(jnp.bfloat16)
            rest = rest - piece.astype(jnp.float32)
            got = lax.dot_general(piece, pick, (((0,), (0,)), ((), ())), preferred_element_type=jnp.float32)
            total = got if total is None else total + got
        out_ref[pl.ds(part, 1), :] = jnp.sum(jnp.where(here, total, 0.0), axis=0, keepdims=True)


def station_weights(obliquity, stations):
    parts, line = obliquity.shape
    table = obliquity.reshape(parts, line // LANES, LANES).transpose(1, 0, 2)
    count = stations.shape[0]
    return pl.pallas_call(
        weights_kernel,
        in_specs=[pl.BlockSpec(memory_space=pltpu.VMEM), ANY],
        out_specs=pl.BlockSpec(memory_space=pltpu.VMEM),
        out_shape=jax.ShapeDtypeStruct((parts, count), jnp.float32),
        scratch_shapes=[pltpu.VMEM((parts, line // LANES, LANES), jnp.float32), pltpu.SemaphoreType.DMA((parts,))],
        compiler_params=pltpu.CompilerParams(vmem_limit_bytes=32 * 2**20),
        cost_estimate=pl.CostEstimate(flops=12 * line * count, bytes_accessed=4 * parts * line, transcendentals=0),
    )(stations[None, :], table)


def tiles_kernel(places, form, unroll, rows_ref, cols_ref, valid_ref, at_ref, *refs):
    n = len(places)
    pieces = refs[: 2 * n]
    weight_ref = refs[2 * n]
    refs = refs[2 * n + 1 :]
    acc_ref = None
    got_refs = ()
    if form == "start":
        _, out_ref, token_ref = refs
    elif form == "last":
        acc_ref, *got_refs, _, result_ref, out_ref, sem = refs
    else:
        acc_ref, _, *outs, token_ref = refs
        out_ref = outs[0]
    if form != "last":
        token_ref[...] = jnp.zeros_like(token_ref)
    slots = rows_ref.shape[0]
    side = out_ref.shape[2]
    per_half = pieces[0].shape[0] // side
    rcv = at_ref[0]
    shard = at_ref[1]
    half_lane = lax.broadcasted_iota(jnp.int32, (1, LANES), 1) < LANES // 2
    sign = jnp.where(half_lane, 1.0, -1.0).astype(jnp.bfloat16)
    w_at = [lax.bitwise_xor(shard, relative) * 2 + lax.bitwise_xor(rcv, other) for relative, other in places]
    w_real = [weight_ref[0, pl.ds(index, 1), :] for index in w_at]
    w_imag = [weight_ref[1, pl.ds(index, 1), :] for index in w_at]

    def panel(piece, tile):
        place = pl.ds(pl.multiple_of(lax.rem(tile, per_half) * side, side), side)
        return jnp.where(tile // per_half == rcv, pieces[2 * piece][place, :], pieces[2 * piece + 1][place, :])

    def one_slot(slot, step, i):
        row = rows_ref[slot]
        col = cols_ref[slot]
        scale = -valid_ref[slot].astype(jnp.float32)
        both = None
        for first in range(0, n, GROUP):
            upper, lower, right = [], [], []
            for p in range(first, min(first + GROUP, n)):
                value = panel(p, row).astype(jnp.float32)
                weighted = value * (scale * w_real[p]) + pltpu.roll(value, LANES // 2, 1) * (scale * w_imag[p])
                weighted = weighted.astype(jnp.bfloat16)
                upper.append(weighted * sign)
                lower.append(pltpu.roll(weighted, LANES // 2, 1))
                right.append(panel(p, col))
            left = jnp.concatenate([jnp.concatenate(upper, 1), jnp.concatenate(lower, 1)], 0)
            part = lax.dot_general(
                left, jnp.concatenate(right, 1), (((1,), (1,)), ((), ())), preferred_element_type=jnp.float32
            )
            both = part if both is None else both + part
        for part in range(2):
            value = both[part * side : (part + 1) * side]
            if acc_ref is not None:
                value = acc_ref[slot, part] + value
            if got_refs:
                value = value + got_refs[i][step, part].astype(jnp.float32)
            if form == "give":
                outs[i][step, part] = value.astype(out_ref.dtype)
            else:
                out_ref[slot, part] = value
        if form == "last":
            pltpu.make_async_copy(out_ref.at[slot], result_ref.at[slot], sem.at[slot]).start()

    steps = slots // unroll

    group = unroll // 2 if form == "last" and unroll > 1 else unroll
    for base in range(0, unroll, group):

        @pl.loop(0, steps)
        def _(step):
            for i in range(base, base + group):
                one_slot(i * steps + step, step, i)

    if form == "last":

        @pl.loop(0, slots)
        def _(slot):
            pltpu.make_async_copy(out_ref.at[slot], result_ref.at[slot], sem.at[slot]).wait()


def subtract(form, pieces, scalars, weights, shape, token, acc=None, got=()):
    n = len(pieces)
    places = [piece[:2] for piece in pieces]
    operands = [array for piece in pieces for array in piece[2:]] + [weights]
    operands += ([] if acc is None else [acc]) + list(got) + [token]
    vmem = pl.BlockSpec(memory_space=pltpu.VMEM)
    last = form == "last"
    unroll = 8 if shape[0] % 8 == 0 else 1
    result = jax.ShapeDtypeStruct(shape, jnp.float32)
    if form == "give":
        result = [jax.ShapeDtypeStruct((shape[0] // unroll,) + shape[1:], jnp.bfloat16)] * unroll
    elif not last:
        result = pltpu.VMEM(shape, jnp.float32)
    return pl.pallas_call(
        functools.partial(tiles_kernel, places, form, unroll),
        in_specs=[pl.BlockSpec(memory_space=pltpu.SMEM)] * 4 + [vmem] * len(operands),
        out_specs=ANY if last else [vmem] * (1 + (unroll if form == "give" else 1)),
        scratch_shapes=[pltpu.VMEM(shape, jnp.float32), pltpu.SemaphoreType.DMA((shape[0],))] if last else [],
        out_shape=result if last else [*(result if form == "give" else [result]), jax.ShapeDtypeStruct((8, LANES), jnp.float32)],
        input_output_aliases={4 + 2 * n + 1: 0} if form == "add" else {},
        compiler_params=pltpu.CompilerParams(vmem_limit_bytes=LIMIT * 2**20),
        cost_estimate=pl.CostEstimate(flops=COST, bytes_accessed=COST, transcendentals=0),
    )(*scalars, *operands)


def body(panel, obliquity, panel_stations, tile_map, recorded):
    n_src = lax.axis_size("src")
    n_rcv = lax.axis_size("rcv")
    rcv = lax.axis_index("rcv")
    src = lax.axis_index("src")
    slots = recorded.shape[0]
    shards = 8
    span = n_src // shards
    if span > 1:
        groups = [[g * span + i for i in range(span)] for g in range(shards)]
        near = lax.all_gather(panel.astype(jnp.bfloat16), "src", axis=1, tiled=True, axis_index_groups=groups)
        panel = near.astype(jnp.float32)

    def send(a, distance):
        return lax.ppermute(a, "src", [(i, i ^ (distance * span)) for i in range(n_src)])

    def swap(a):
        return lax.ppermute(a, "rcv", [(0, 1), (1, 0)])

    def slots_of(device):
        mine = lax.dynamic_slice_in_dim(tile_map, device * slots, slots, 0)
        valid = (mine[:, 0] >= 0).astype(jnp.int32)
        place = jnp.stack([rcv, src // span]).astype(jnp.int32)
        return jnp.maximum(mine[:, 0], 0), jnp.maximum(mine[:, 1], 0), valid, place

    mine = slots_of(src * n_rcv + rcv)
    theirs = slots_of(src * n_rcv + 1 - rcv)
    w = station_weights(obliquity, panel_stations).reshape(2, shards * 2, -1)
    weights = jnp.stack([jnp.concatenate([w[0], w[0]], -1), jnp.concatenate([-w[1], w[1]], -1)])
    shape = recorded.shape
    token = jnp.zeros((8, LANES), jnp.float32)

    X, Z1, Z2 = 1, 2, 4
    h0, give = turn(panel, rcv)
    h1 = swap(give)
    A0 = send(h0, Z1)
    B0 = send(h0, Z2)
    X0 = send(h0, X)
    X1 = send(h1, X)
    A0, B0, X0, X1, weights = together((A0, B0, X0, X1, weights))

    A1 = send(h1, Z1)
    B1 = send(h1, Z2)
    XA0 = send(A0, X)
    XB0 = send(B0, X)
    pieces = [(0, 0, h0, h1), (X, 0, X0, X1)]
    away, token = subtract("start", pieces, theirs, weights, shape, token)
    home, token = subtract("first", pieces, mine, weights, shape, token, recorded)
    A1, B1, XA0, XB0, token = together((A1, B1, XA0, XB0, token))

    ZZ0 = send(B0, Z1)
    ZZ1 = send(B1, Z1)
    XB1 = send(B1, X)
    XA1 = send(A1, X)
    pieces = [(Z1, 0, A0, A1), (Z2, 0, B0, B1), (X + Z2, 0, XB0, XB1)]
    away, token = subtract("add", pieces, theirs, weights, shape, token, away)
    home, token = subtract("add", pieces, mine, weights, shape, token, home)
    ZZ1, XA1, token = together((ZZ1, XA1, token))

    XZZ0 = send(ZZ0, X)
    ZXB1 = send(XB1, Z1)
    pieces = [(Z1 + Z2, 0, ZZ0, ZZ1), (X + Z1, 0, XA0, XA1)]
    home, token = subtract("add", pieces, mine, weights, shape, token, home)
    *away, token = subtract("give", pieces, theirs, weights, shape, token, away)
    got = [swap(a) for a in away]
    XZZ0, ZXB1, token = together((XZZ0, ZXB1, token))

    far = X + Z1 + Z2
    pieces = [(far, 0, XZZ0, ZXB1), (far, 1, swap(ZXB1), swap(XZZ0))]
    return subtract("last", pieces, mine, weights, shape, token, home, got)


def solution(mesh):
    return jax.shard_map(
        body,
        mesh=mesh,
        in_specs=(
            P("freq", "src", "rcv"),
            P("freq", None),
            P(),
            P("freq", None),
            P(("src", "rcv"), "freq", None, None),
        ),
        out_specs=P(("src", "rcv"), "freq", None, None),
        check_vma=False,
    )
```

```python
import functools

import jax
import jax.numpy as jnp
from jax import lax
from jax.experimental import pallas as pl
from jax.experimental.pallas import tpu as pltpu
from jax.sharding import PartitionSpec as P

LANES = 128
GROUPS = (2, 2, 2, 1, 1)
COST = 1000
LIMIT = 16
GROUP = 2
ANY = pl.BlockSpec(memory_space=pl.ANY)
together = lax.optimization_barrier


def turn_kernel(_, kept_in, given_in, kept_out, given_out):
    for in_ref, out_ref in ((kept_in, kept_out), (given_in, given_out)):
        block = in_ref[...]
        out_ref[...] = block.reshape(block.shape[0] * block.shape[1], block.shape[2]).T.astype(jnp.bfloat16)


def turn(panel, rcv):
    parts, depth, width = panel.shape
    depth = depth // 2
    cols = width // 2
    out = jax.ShapeDtypeStruct((width, parts * depth), jnp.bfloat16)
    return pl.pallas_call(
        turn_kernel,
        grid_spec=pltpu.PrefetchScalarGridSpec(
            num_scalar_prefetch=1,
            grid=(width // cols,),
            in_specs=[
                pl.BlockSpec((parts, depth, cols), lambda c, r: (0, r[0], c)),
                pl.BlockSpec((parts, depth, cols), lambda c, r: (0, 1 - r[0], c)),
            ],
            out_specs=[pl.BlockSpec((cols, parts * depth), lambda c, r: (c, 0))] * 2,
        ),
        out_shape=[out, out],
        cost_estimate=pl.CostEstimate(flops=0, bytes_accessed=6 * panel.size, transcendentals=0),
    )(rcv[None], panel, panel)


def weights_kernel(stations_ref, line_ref, out_ref, table, sem):
    copies = [pltpu.make_async_copy(line_ref.at[:, part], table.at[part], sem.at[part]) for part in range(2)]
    for copy in copies:
        copy.start()
    stations = stations_ref[...]
    n_blocks = table.shape[1]
    block = lax.broadcasted_iota(jnp.int32, (n_blocks, stations.shape[1]), 0)
    pick = (block == stations // LANES).astype(jnp.float32).astype(jnp.bfloat16)
    lane = lax.broadcasted_iota(jnp.int32, (LANES, stations.shape[1]), 0)
    here = lane == stations % LANES
    for part in range(2):
        copies[part].wait()
        rest = table[part]
        total = None
        for _ in range(3):
            piece = rest.astype(jnp.bfloat16)
            rest = rest - piece.astype(jnp.float32)
            got = lax.dot_general(piece, pick, (((0,), (0,)), ((), ())), preferred_element_type=jnp.float32)
            total = got if total is None else total + got
        out_ref[pl.ds(part, 1), :] = jnp.sum(jnp.where(here, total, 0.0), axis=0, keepdims=True)


def station_weights(obliquity, stations):
    parts, line = obliquity.shape
    table = obliquity.reshape(parts, line // LANES, LANES).transpose(1, 0, 2)
    count = stations.shape[0]
    return pl.pallas_call(
        weights_kernel,
        in_specs=[pl.BlockSpec(memory_space=pltpu.VMEM), ANY],
        out_specs=pl.BlockSpec(memory_space=pltpu.VMEM),
        out_shape=jax.ShapeDtypeStruct((parts, count), jnp.float32),
        scratch_shapes=[pltpu.VMEM((parts, line // LANES, LANES), jnp.float32), pltpu.SemaphoreType.DMA((parts,))],
        compiler_params=pltpu.CompilerParams(vmem_limit_bytes=32 * 2**20),
        cost_estimate=pl.CostEstimate(flops=12 * line * count, bytes_accessed=4 * parts * line, transcendentals=0),
    )(stations[None, :], table)


def groups_of(count):
    return GROUPS if count == sum(GROUPS) else (1,) * count


def tiles_kernel(places, form, unroll, first_got, rows_ref, cols_ref, valid_ref, at_ref, *refs):
    n = len(places)
    pieces = refs[: 2 * n]
    weight_ref = refs[2 * n]
    refs = refs[2 * n + 1 :]
    acc_ref = None
    got_refs = ()
    if form == "start":
        _, out_ref, token_ref = refs
    elif form == "last":
        acc_ref, *got_refs, _, result_ref, out_ref, sem = refs
    elif form == "give":
        acc_ref, _, *outs, token_ref = refs
        out_ref = outs[0]
    else:
        acc_ref, *got_refs, _, out_ref, token_ref = refs
    if form != "last":
        token_ref[...] = jnp.zeros_like(token_ref)
    slots = rows_ref.shape[0]
    side = out_ref.shape[2]
    per_half = pieces[0].shape[0] // side
    rcv = at_ref[0]
    shard = at_ref[1]
    half_lane = lax.broadcasted_iota(jnp.int32, (1, LANES), 1) < LANES // 2
    sign = jnp.where(half_lane, 1.0, -1.0).astype(jnp.bfloat16)
    w_at = [lax.bitwise_xor(shard, relative) * 2 + lax.bitwise_xor(rcv, other) for relative, other in places]
    w_real = [weight_ref[0, pl.ds(index, 1), :] for index in w_at]
    w_imag = [weight_ref[1, pl.ds(index, 1), :] for index in w_at]

    def panel(piece, tile):
        place = pl.ds(pl.multiple_of(lax.rem(tile, per_half) * side, side), side)
        return jnp.where(tile // per_half == rcv, pieces[2 * piece][place, :], pieces[2 * piece + 1][place, :])

    def one_slot(slot, step, i):
        row = rows_ref[slot]
        col = cols_ref[slot]
        scale = -valid_ref[slot].astype(jnp.float32)
        both = None
        for first in range(0, n, GROUP):
            upper, lower, right = [], [], []
            for p in range(first, min(first + GROUP, n)):
                value = panel(p, row).astype(jnp.float32)
                weighted = value * (scale * w_real[p]) + pltpu.roll(value, LANES // 2, 1) * (scale * w_imag[p])
                weighted = weighted.astype(jnp.bfloat16)
                upper.append(weighted * sign)
                lower.append(pltpu.roll(weighted, LANES // 2, 1))
                right.append(panel(p, col))
            left = jnp.concatenate([jnp.concatenate(upper, 1), jnp.concatenate(lower, 1)], 0)
            part = lax.dot_general(
                left, jnp.concatenate(right, 1), (((1,), (1,)), ((), ())), preferred_element_type=jnp.float32
            )
            both = part if both is None else both + part
        for part in range(2):
            value = both[part * side : (part + 1) * side]
            if acc_ref is not None:
                value = acc_ref[slot, part] + value
            o, at = where[i]
            if 0 <= o - first_got < len(got_refs):
                value = value + got_refs[o - first_got][at * steps + step, part].astype(jnp.float32)
            if form == "give":
                o, at = where[i]
                outs[o][at * steps + step, part] = value.astype(out_ref.dtype)
            else:
                out_ref[slot, part] = value
        if form == "last":
            pltpu.make_async_copy(out_ref.at[slot], result_ref.at[slot], sem.at[slot]).start()

    steps = slots // unroll
    where = [(o, at) for o, g in enumerate(groups_of(unroll)) for at in range(g)]

    group = unroll // 2 if form == "last" and unroll > 1 else unroll
    for base in range(0, unroll, group):

        @pl.loop(0, steps)
        def _(step):
            for i in range(base, base + group):
                one_slot(i * steps + step, step, i)

    if form == "last":

        @pl.loop(0, slots)
        def _(slot):
            pltpu.make_async_copy(out_ref.at[slot], result_ref.at[slot], sem.at[slot]).wait()


def subtract(form, pieces, scalars, weights, shape, token, acc=None, got=(), first_got=0):
    n = len(pieces)
    places = [piece[:2] for piece in pieces]
    operands = [array for piece in pieces for array in piece[2:]] + [weights]
    operands += ([] if acc is None else [acc]) + list(got) + [token]
    vmem = pl.BlockSpec(memory_space=pltpu.VMEM)
    last = form == "last"
    unroll = 8 if shape[0] % 8 == 0 else 1
    result = jax.ShapeDtypeStruct(shape, jnp.float32)
    if form == "give":
        result = [jax.ShapeDtypeStruct((shape[0] // unroll * g,) + shape[1:], jnp.bfloat16) for g in groups_of(unroll)]
    elif not last:
        result = pltpu.VMEM(shape, jnp.float32)
    return pl.pallas_call(
        functools.partial(tiles_kernel, places, form, unroll, first_got),
        in_specs=[pl.BlockSpec(memory_space=pltpu.SMEM)] * 4 + [vmem] * len(operands),
        out_specs=ANY if last else [vmem] * (1 + (len(result) if form == "give" else 1)),
        scratch_shapes=[pltpu.VMEM(shape, jnp.float32), pltpu.SemaphoreType.DMA((shape[0],))] if last else [],
        out_shape=result if last else [*(result if form == "give" else [result]), jax.ShapeDtypeStruct((8, LANES), jnp.float32)],
        input_output_aliases={4 + 2 * n + 1: 0} if form == "add" else {},
        compiler_params=pltpu.CompilerParams(vmem_limit_bytes=LIMIT * 2**20),
        cost_estimate=pl.CostEstimate(flops=COST, bytes_accessed=COST, transcendentals=0),
    )(*scalars, *operands)


def body(panel, obliquity, panel_stations, tile_map, recorded):
    n_src = lax.axis_size("src")
    n_rcv = lax.axis_size("rcv")
    rcv = lax.axis_index("rcv")
    src = lax.axis_index("src")
    slots = recorded.shape[0]
    shards = 8
    span = n_src // shards
    if span > 1:
        groups = [[g * span + i for i in range(span)] for g in range(shards)]
        near = lax.all_gather(panel.astype(jnp.bfloat16), "src", axis=1, tiled=True, axis_index_groups=groups)
        panel = near.astype(jnp.float32)

    def send(a, distance):
        return lax.ppermute(a, "src", [(i, i ^ (distance * span)) for i in range(n_src)])

    def swap(a):
        return lax.ppermute(a, "rcv", [(0, 1), (1, 0)])

    def slots_of(device):
        mine = lax.dynamic_slice_in_dim(tile_map, device * slots, slots, 0)
        valid = (mine[:, 0] >= 0).astype(jnp.int32)
        place = jnp.stack([rcv, src // span]).astype(jnp.int32)
        return jnp.maximum(mine[:, 0], 0), jnp.maximum(mine[:, 1], 0), valid, place

    mine = slots_of(src * n_rcv + rcv)
    theirs = slots_of(src * n_rcv + 1 - rcv)
    w = station_weights(obliquity, panel_stations).reshape(2, shards * 2, -1)
    weights = jnp.stack([jnp.concatenate([w[0], w[0]], -1), jnp.concatenate([-w[1], w[1]], -1)])
    shape = recorded.shape
    token = jnp.zeros((8, LANES), jnp.float32)

    X, Z1, Z2 = 1, 2, 4
    h0, give = turn(panel, rcv)
    h1 = swap(give)
    B0 = send(h0, Z2)
    X0 = send(h0, X)
    A0 = send(h0, Z1)
    X1 = send(h1, X)
    A0, B0, X0, X1, weights = together((A0, B0, X0, X1, weights))

    A1 = send(h1, Z1)
    B1 = send(h1, Z2)
    XA0 = send(A0, X)
    XB0 = send(B0, X)
    pieces = [(0, 0, h0, h1), (X, 0, X0, X1)]
    away, token = subtract("start", pieces, theirs, weights, shape, token)
    home, token = subtract("first", pieces, mine, weights, shape, token, recorded)
    A1, B1, XA0, XB0, token = together((A1, B1, XA0, XB0, token))

    ZZ0 = send(B0, Z1)
    ZZ1 = send(B1, Z1)
    XB1 = send(B1, X)
    XA1 = send(A1, X)
    pieces = [(Z1, 0, A0, A1), (Z2, 0, B0, B1), (X + Z2, 0, XB0, XB1)]
    away, token = subtract("add", pieces, theirs, weights, shape, token, away)
    home, token = subtract("add", pieces, mine, weights, shape, token, home)
    ZZ1, XA1, token = together((ZZ1, XA1, token))

    XZZ0 = send(ZZ0, X)
    ZXB1 = send(XB1, Z1)
    pieces = [(Z1 + Z2, 0, ZZ0, ZZ1), (X + Z1, 0, XA0, XA1)]
    home, token = subtract("add", pieces, mine, weights, shape, token, home)
    *away, token = subtract("give", pieces, theirs, weights, shape, token, away)
    got = [swap(a) for a in away]
    XZZ0, ZXB1, token = together((XZZ0, ZXB1, token))

    far = X + Z1 + Z2
    home, token = subtract("add", [(far, 0, XZZ0, ZXB1)], mine, weights, shape, token, home, got[:0])
    return subtract("last", [(far, 1, swap(ZXB1), swap(XZZ0))], mine, weights, shape, token, home, got[0:], 0)


def solution(mesh):
    return jax.shard_map(
        body,
        mesh=mesh,
        in_specs=(
            P("freq", "src", "rcv"),
            P("freq", None),
            P(),
            P("freq", None),
            P(("src", "rcv"), "freq", None, None),
        ),
        out_specs=P(("src", "rcv"), "freq", None, None),
        check_vma=False,
    )
```
